32 devices in a mesh: box: 8 (over y, x, core), dir: 4 (over z).
Axes of the slice: x: 2, y: 2, z: 4, core: 2. Of those that a mesh axis runs over, the one named last changes fastest.
Arguments:
- fine_out: float32 [1024, 2, 8192], P(('box', 'dir')), may hold values from -6 to 6
- theta_interp: float32 [128, 64], replicated, may hold values from -0.75 to 0.75
- phi_interp: float32 [128, 256], replicated, may hold values from -0.5 to 0.5
- shift_phase: float32 [8, 32768], P(None, 'dir'), may hold values from -3.140625 to 3.140625
- translation: float32 [316, 2, 32768], P(None, None, 'dir'), may hold values from -0.25 to 0.25
- upper_in: float32 [128, 2, 32768], P('box', None, 'dir'), may hold values from -6 to 6
- children: int32 [128, 8], P('box'), may hold values from 0 to 1023, as said below
- far_boxes: int32 [128, 28], P('box'), may hold values from 0 to 127, as said below
- far_offsets: int32 [128, 28], P('box'), may hold values from 0 to 315
Outputs:
- coarse_in: float32 [128, 2, 32768], P('box', None, 'dir')
- fine_in: float32 [1024, 2, 8192], P(('box', 'dir'))
The draws below stay inside these ranges and needn't reach their ends.
Inputs may be any that keep to these rules, and one draw needn't show every extreme that they name: Every fine box is named exactly once. The coarse boxes i * 16 to (i + 1) * 16 - 1 have as children exactly the fine boxes 8 * i * 16 to 8 * (i + 1) * 16 - 1. `far_boxes`: each row names 28 different coarse boxes, never the row's own box.
All inputs are finite; a program needn't handle non-finite values.
Results may differ from the reference program's by a relative error of at most 0.00008.
Values sent between devices are 32-bit elements; how exact they have to be, the bound alone decides.
A program may use at most 192 MiB of HBM per device.

```python
import jax
import jax.numpy as jnp
from jax import lax

TC = 128
PC = 256
TF = 64
PF = 128
NOFF = 316
LIST = 28
BOX_DEV = 16
KC = 32768
KF = 8192
BC = 128
BF = 1024


def draw_children(key, part):
    groups = BC // BOX_DEV
    span_rows = 8 * BOX_DEV
    scores = jax.random.randint(key, (groups, span_rows), 0, 1 << 20) * span_rows + jnp.arange(span_rows)[None, :]
    order = jnp.argsort(scores, axis=1)
    placed = order + (jnp.arange(groups) * span_rows)[:, None]
    return placed.reshape(BC, 8).astype(jnp.int32)


def draw_far_boxes(key, part):
    scores = jax.random.randint(key, (BC, BC - 1), 0, 1 << 20) * BC + jnp.arange(BC - 1)[None, :]
    order = jnp.argsort(scores, axis=1)[:, :LIST]
    own_box = jnp.arange(BC)[:, None]
    return (order + (order >= own_box).astype(order.dtype)).astype(jnp.int32)


def set_ends(array, stream_key, smallest, largest):
    longest = array.shape.index(max(array.shape))
    spots = []
    for shift in (0, 1):
        where = [jax.random.randint(jax.random.fold_in(stream_key, axis), (), 0, length) for axis, length in enumerate(array.shape)]
        where[longest] = (where[longest] + shift) % array.shape[longest]
        spots.append(tuple(where))
    return array.at[spots[0]].set(smallest).at[spots[1]].set(largest)


def levels(stream_key, dims, cuts, smallest, largest):
    factor_of = 1.0
    for position, blocks in cuts:
        heights = jax.random.uniform(jax.random.fold_in(jax.random.fold_in(stream_key, 6), position), (blocks,), jnp.float32, smallest / len(cuts), largest / len(cuts))
        factor_of = factor_of * jnp.repeat(jnp.exp(heights), dims[position] // blocks).reshape((-1,) + (1,) * (len(dims) - 1 - position))
    return factor_of


def normal_values(rng, dims, scale, limit, split=(), held_as=jnp.bfloat16):
    factor_of = levels(rng, dims, split, -0.22, 0.18) if split else 1.0
    array = jax.random.normal(rng, dims, jnp.float32) * scale * factor_of
    return jnp.minimum(jnp.maximum(array, -limit), limit).astype(held_as)


def setup_inputs(seed: int = 0) -> dict:
    key_list = jax.random.split(jax.random.key(seed), 10)
    return {
        "fine_out": normal_values(key_list[0], (BF, 2, KF), 1.0, 6.0, ((0, 32),), jnp.float32),
        "theta_interp": normal_values(key_list[1], (TC, TF), TF ** -0.5, 0.75, (), jnp.float32),
        "phi_interp": normal_values(key_list[2], (PF, PC), PF ** -0.5, 0.5, (), jnp.float32),
        "shift_phase": jnp.clip(jax.random.uniform(key_list[3], (8, KC), jnp.float32, -3.140625, 3.140625), -3.140625, 3.140625),
        "translation": normal_values(key_list[4], (NOFF, 2, KC), (16 * LIST) ** -0.5, 0.25, ((2, 4),), jnp.float32),
        "upper_in": normal_values(key_list[5], (BC, 2, KC), 1.0, 6.0, ((0, 8), (2, 4)), jnp.float32),
        "children": draw_children(jax.random.fold_in(key_list[9], 71), 0),
        "far_boxes": draw_far_boxes(jax.random.fold_in(key_list[9], 71), 0),
        "far_offsets": set_ends(jax.random.randint(key_list[8], (BC, LIST), 0, NOFF), jax.random.fold_in(key_list[8], 1), 0, NOFF - 1).astype(jnp.int32),
    }


HIGHEST_PREC = lax.Precision.HIGHEST


def interpolate(patterns, theta_map, phi_map):
    amount = patterns.shape[0]
    coarse_theta, fine_theta = theta_map.shape
    fine_phi, coarse_phi = phi_map.shape
    flat_rows = patterns.reshape(amount * 2 * fine_theta, fine_phi)
    along_phi = jnp.dot(flat_rows, phi_map, precision=HIGHEST_PREC, preferred_element_type=jnp.float32)
    along_phi = along_phi.reshape(amount, 2, fine_theta, coarse_phi)
    result = jnp.einsum("tu,ncus->ncts", theta_map, along_phi, precision=HIGHEST_PREC)
    return result.reshape(amount, 2, coarse_theta * coarse_phi)


def anterpolate(patterns, theta_map, phi_map):
    amount = patterns.shape[0]
    coarse_theta, fine_theta = theta_map.shape
    fine_phi, coarse_phi = phi_map.shape
    flat_rows = patterns.reshape(amount * 2 * coarse_theta, coarse_phi)
    along_phi = jnp.dot(flat_rows, phi_map.T, precision=HIGHEST_PREC, preferred_element_type=jnp.float32)
    along_phi = along_phi.reshape(amount, 2, coarse_theta, fine_phi)
    result = jnp.einsum("tu,ncts->ncus", theta_map, along_phi, precision=HIGHEST_PREC)
    return result.reshape(amount, 2, fine_theta * fine_phi)


def aggregate(child_rows, child_index, cosine, sine):
    picked = child_rows[child_index]
    real_part = jnp.sum(cosine * picked[:, :, 0] - sine * picked[:, :, 1], axis=1)
    imag_part = jnp.sum(sine * picked[:, :, 0] + cosine * picked[:, :, 1], axis=1)
    return jnp.stack([real_part, imag_part], axis=1)


def disaggregate(incoming, child_index, cosine, sine, total):
    real_in = incoming[:, None, 0]
    imag_in = incoming[:, None, 1]
    real_part = cosine * real_in + sine * imag_in
    imag_part = cosine * imag_in - sine * real_in
    width = incoming.shape[2]
    values = jnp.stack([real_part, imag_part], axis=2).reshape(-1, 2, width)
    empty = jnp.zeros((total, 2, width), jnp.float32)
    return empty.at[child_index.reshape(-1)].set(values)


def reference(fine_out, theta_interp, phi_interp, shift_phase, translation, upper_in, children, far_boxes, far_offsets):
    cosine = jnp.cos(shift_phase)
    sine = jnp.sin(shift_phase)
    child_rows = interpolate(fine_out, theta_interp, phi_interp)
    outgoing = aggregate(child_rows, children, cosine, sine)

    def translate_one(entry):
        far_index, far_kind = entry
        source_rows = outgoing[far_index]
        kernel_rows = translation[far_kind]
        real_part = jnp.sum(kernel_rows[:, 0] * source_rows[:, 0] - kernel_rows[:, 1] * source_rows[:, 1], axis=0)
        imag_part = jnp.sum(kernel_rows[:, 0] * source_rows[:, 1] + kernel_rows[:, 1] * source_rows[:, 0], axis=0)
        return jnp.stack([real_part, imag_part], axis=0)

    translated = lax.map(translate_one, (far_boxes, far_offsets))
    coarse_in = translated + upper_in
    child_in = disaggregate(coarse_in, children, cosine, sine, fine_out.shape[0])
    fine_in = anterpolate(child_in, theta_interp, phi_interp)
    return coarse_in, fine_in
```

```python
import functools

import jax
import jax.numpy as jnp
from jax import lax
from jax.experimental import pallas as pl
from jax.experimental.pallas import tpu as pltpu
from jax.sharding import PartitionSpec as P

F32, BF16 = jnp.float32, jnp.bfloat16
VMEM_BYTES = 52 * 1024 * 1024


def split(x):
    hi = x.astype(BF16)
    return hi, (x - hi.astype(F32)).astype(BF16)


def dot3(a, b):
    (ah, al), (bh, bl) = a, b
    d = functools.partial(jnp.dot, preferred_element_type=F32)
    return d(ah, bh) + (d(ah, bl) + d(al, bh))


def rows_view(x):
    n, _, k = x.shape
    return x.reshape(n, 2, k // 128, 128).transpose(0, 2, 1, 3).reshape(n, k // 64, 128)


def rows_unview(x):
    n, r, _ = x.shape
    return x.reshape(n, r // 2, 2, 128).transpose(0, 2, 1, 3).reshape(n, 2, r * 64)


def gather_up_kernel(group, parent, octant, x_ref, theta_ref, phi_ref, cs_ref, out_ref):
    step = pl.program_id(0)
    nd, tl = out_ref.shape[0], out_ref.shape[3]
    tc = nd * tl

    @pl.when(step == 0)
    def _():
        out_ref[...] = jnp.zeros_like(out_ref)

    theta = split(theta_ref[...])
    phi = split(phi_ref[...])
    rows = x_ref.shape[1]
    along = dot3(split(x_ref[...].reshape(group * rows, x_ref.shape[2])), phi)
    for g in range(group):
        p, o = parent[step * group + g], octant[step * group + g]
        full = dot3(theta, split(along[g * rows : (g + 1) * rows]))
        for j in range(nd):
            re = full[j * tl : (j + 1) * tl]
            im = full[tc + j * tl : tc + (j + 1) * tl]
            c, s = cs_ref[j, 0, o], cs_ref[j, 1, o]
            out_ref[j, p, 0] += c * re - s * im
            out_ref[j, p, 1] += s * re + c * im


def gather_up(x, theta2, phi, cs, parent, octant, parents):
    n, rows, lanes = x.shape
    nd, _, _, tl, pc = cs.shape
    group = 4
    return pl.pallas_call(
        functools.partial(gather_up_kernel, group),
        grid_spec=pltpu.PrefetchScalarGridSpec(
            num_scalar_prefetch=2,
            grid=(n // group,),
            in_specs=[
                pl.BlockSpec((group, rows, lanes), lambda i, *_: (i, 0, 0)),
                pl.BlockSpec(theta2.shape, lambda i, *_: (0, 0)),
                pl.BlockSpec(phi.shape, lambda i, *_: (0, 0)),
                pl.BlockSpec(cs.shape, lambda i, *_: (0, 0, 0, 0, 0)),
            ],
            out_specs=pl.BlockSpec((nd, parents, 2, tl, pc), lambda i, *_: (0, 0, 0, 0, 0)),
        ),
        out_shape=jax.ShapeDtypeStruct((nd, parents, 2, tl, pc), F32),
        compiler_params=pltpu.CompilerParams(vmem_limit_bytes=VMEM_BYTES),
    )(parent, octant, x, theta2, phi, cs)


def translate_kernel(far, kind, q_ref, trans_ref, upper_ref, rows_ref, plane_ref, buf, sem):
    p = pl.program_id(0)
    count, many = pl.num_programs(0), far.shape[1]
    tl = q_ref.shape[2]

    def start(row, slot):
        for l in range(many):
            pltpu.make_async_copy(trans_ref.at[kind[row, l]], buf.at[slot, l], sem.at[slot]).start()

    @pl.when(p == 0)
    def _():
        start(0, 0)

    @pl.when(p + 1 < count)
    def _():
        start(p + 1, (p + 1) % 2)

    slot = p % 2
    pltpu.make_async_copy(trans_ref.at[pl.ds(0, many)], buf.at[slot], sem.at[slot]).wait()
    for t in range(0, tl, 8):
        for h in range(2):
            re = im = None
            for l in range(many):
                f = far[p, l]
                q0 = q_ref[f, 0, t : t + 8, h * 128 : (h + 1) * 128]
                q1 = q_ref[f, 1, t : t + 8, h * 128 : (h + 1) * 128]
                a0 = buf[slot, l, pl.ds(t * 4 + h * 2, 8, stride=4), :]
                a1 = buf[slot, l, pl.ds(t * 4 + h * 2 + 1, 8, stride=4), :]
                r, i = a0 * q0 - a1 * q1, a0 * q1 + a1 * q0
                re = r if re is None else re + r
                im = i if im is None else im + i
            for c, total in ((0, re), (1, im)):
                where = pl.ds(t * 4 + h * 2 + c, 8, stride=4)
                total = total + upper_ref[0, where, :]
                rows_ref[0, where, :] = total
                plane_ref[0, c, t : t + 8, h * 128 : (h + 1) * 128] = total


def translate(q, trans, upper, far, kind):
    parents, rows, lanes = upper.shape
    _, _, tl, pc = q.shape
    many = far.shape[1]
    return pl.pallas_call(
        translate_kernel,
        grid_spec=pltpu.PrefetchScalarGridSpec(
            num_scalar_prefetch=2,
            grid=(parents,),
            in_specs=[
                pl.BlockSpec(q.shape, lambda i, *_: (0, 0, 0, 0)),
                pl.BlockSpec(memory_space=pl.ANY),
                pl.BlockSpec((1, rows, lanes), lambda i, *_: (i, 0, 0)),
            ],
            out_specs=[
                pl.BlockSpec((1, rows, lanes), lambda i, *_: (i, 0, 0)),
                pl.BlockSpec((1, 2, tl, pc), lambda i, *_: (i, 0, 0, 0)),
            ],
            scratch_shapes=[
                pltpu.VMEM((2, many, rows, lanes), F32),
                pltpu.SemaphoreType.DMA((2,)),
            ],
        ),
        out_shape=[
            jax.ShapeDtypeStruct((parents, rows, lanes), F32),
            jax.ShapeDtypeStruct((parents, 2, tl, pc), F32),
        ],
        compiler_params=pltpu.CompilerParams(vmem_limit_bytes=VMEM_BYTES),
    )(far, kind, q, trans, upper)


def spread_down_kernel(group, parent, octant, in_ref, theta_ref, phi_ref, cs_ref, out_ref, full):
    step = pl.program_id(0)
    nd, tl = in_ref.shape[0], in_ref.shape[3]
    tc = nd * tl
    theta = split(theta_ref[...])
    phi = split(phi_ref[...])
    parts = []
    for g in range(group):
        p, o = parent[step * group + g], octant[step * group + g]
        for j in range(nd):
            re, im = in_ref[j, p, 0], in_ref[j, p, 1]
            c, s = cs_ref[j, 0, o], cs_ref[j, 1, o]
            full[g, j * tl : (j + 1) * tl] = c * re + s * im
            full[g, tc + j * tl : tc + (j + 1) * tl] = c * im - s * re
        parts.append(dot3(theta, split(full[g])))
    along = jnp.concatenate(parts, axis=0)
    out_ref[...] = dot3(split(along), phi).reshape(out_ref.shape)


def spread_down(incoming, theta2t, phit, cs, parent, octant):
    nd, _, _, tl, pc = incoming.shape
    n = parent.shape[0]
    rows, lanes = theta2t.shape[0], phit.shape[1]
    group = 4
    return pl.pallas_call(
        functools.partial(spread_down_kernel, group),
        grid_spec=pltpu.PrefetchScalarGridSpec(
            num_scalar_prefetch=2,
            grid=(n // group,),
            in_specs=[
                pl.BlockSpec(incoming.shape, lambda i, *_: (0, 0, 0, 0, 0)),
                pl.BlockSpec(theta2t.shape, lambda i, *_: (0, 0)),
                pl.BlockSpec(phit.shape, lambda i, *_: (0, 0)),
                pl.BlockSpec(cs.shape, lambda i, *_: (0, 0, 0, 0, 0)),
            ],
            out_specs=pl.BlockSpec((group, rows, lanes), lambda i, *_: (i, 0, 0)),
            scratch_shapes=[pltpu.VMEM((group, 2 * nd * tl, pc), F32)],
        ),
        out_shape=jax.ShapeDtypeStruct((n, rows, lanes), F32),
        compiler_params=pltpu.CompilerParams(vmem_limit_bytes=VMEM_BYTES),
    )(parent, octant, incoming, theta2t, phit, cs)


def shards(
    fine_out,
    theta_interp,
    phi_interp,
    shift_phase,
    translation,
    upper_in,
    children,
    far_boxes,
    far_offsets,
):
    n = fine_out.shape[0]
    tc, tf = theta_interp.shape
    pc = phi_interp.shape[1]
    parents = children.shape[0]
    tl = shift_phase.shape[1] // pc
    nd = tc // tl
    flat = (children % (n * nd)).reshape(-1)
    own = lax.axis_index("dir") * n + jnp.arange(n, dtype=jnp.int32)
    slots = jnp.arange(flat.shape[0], dtype=jnp.int32)
    slot = jnp.sum(jnp.where(flat[None, :] == own[:, None], slots[None, :], 0), axis=1)
    parent, octant = slot // 8, slot % 8
    theta2 = (jnp.eye(2, dtype=F32)[:, None, None, :] * theta_interp[None, :, :, None]).reshape(
        2 * tc, 2 * tf
    )
    phase = shift_phase.reshape(8, tl, pc)
    cs = lax.all_gather(jnp.stack([jnp.cos(phase), jnp.sin(phase)]), "dir", axis=0)
    partial = gather_up(rows_view(fine_out), theta2, phi_interp, cs, parent, octant, parents)
    outgoing = lax.psum_scatter(
        partial.reshape(nd * parents * 2, tl, pc), "dir", scatter_dimension=0, tiled=True
    )
    every_box = lax.all_gather(outgoing.reshape(parents, 2, tl, pc), "box", axis=0, tiled=True)
    rows, planes = translate(
        every_box, rows_view(translation), rows_view(upper_in), far_boxes, far_offsets
    )
    incoming = lax.all_gather(planes, "dir", axis=0)
    fine_in = spread_down(incoming, theta2.T, phi_interp.T, cs, parent, octant)
    return (rows_unview(rows), rows_unview(fine_in))


def solution(mesh):
    placed = (
        P(("box", "dir"), None, None),
        P(),
        P(),
        P(None, "dir"),
        P(None, None, "dir"),
        P("box", None, "dir"),
        P("box", None),
        P("box", None),
        P("box", None),
    )
    return jax.shard_map(
        shards,
        mesh=mesh,
        in_specs=placed,
        out_specs=(P("box", None, "dir"), P(("box", "dir"), None, None)),
        check_vma=False,
    )
```

```python
import functools

import jax
import jax.numpy as jnp
from jax import lax
from jax.experimental import pallas as pl
from jax.experimental.pallas import tpu as pltpu
from jax.sharding import PartitionSpec as P

F32, BF16 = jnp.float32, jnp.bfloat16
VMEM_BYTES = 52 * 1024 * 1024
CHUNKS = 2


def split(x):
    hi = x.astype(BF16)
    return hi, (x - hi.astype(F32)).astype(BF16)


def dot3(a, b):
    (ah, al), (bh, bl) = a, b
    d = functools.partial(jnp.dot, preferred_element_type=F32)
    return d(ah, bh) + (d(ah, bl) + d(al, bh))


def rows_view(x):
    n, _, k = x.shape
    return x.reshape(n, 2, k // 128, 128).transpose(0, 2, 1, 3).reshape(n, k // 64, 128)


def rows_unview(x):
    n, r, _ = x.shape
    return x.reshape(n, r // 2, 2, 128).transpose(0, 2, 1, 3).reshape(n, 2, r * 64)


def gather_up_kernel(group, parent, octant, x_ref, theta_ref, phi_ref, cs_ref, *out_refs):
    step = pl.program_id(0)
    nd, tl = cs_ref.shape[0], cs_ref.shape[3]
    tlc = tl // len(out_refs)
    tc = nd * tl

    @pl.when(step == 0)
    def _():
        for out_ref in out_refs:
            out_ref[...] = jnp.zeros_like(out_ref)

    theta = split(theta_ref[...])
    phi = split(phi_ref[...])
    rows = x_ref.shape[1]
    along = dot3(split(x_ref[...].reshape(group * rows, x_ref.shape[2])), phi)
    for g in range(group):
        p, o = parent[step * group + g], octant[step * group + g]
        full = dot3(theta, split(along[g * rows : (g + 1) * rows]))
        for j in range(nd):
            for h, out_ref in enumerate(out_refs):
                first = j * tl + h * tlc
                re = full[first : first + tlc]
                im = full[tc + first : tc + first + tlc]
                c = cs_ref[j, 0, o, h * tlc : (h + 1) * tlc]
                s = cs_ref[j, 1, o, h * tlc : (h + 1) * tlc]
                out_ref[j, p, 0] += c * re - s * im
                out_ref[j, p, 1] += s * re + c * im


def gather_up(x, theta2, phi, cs, parent, octant, parents):
    n, rows, lanes = x.shape
    nd, _, _, tl, pc = cs.shape
    shape = (nd, parents, 2, tl // CHUNKS, pc)
    group = 4
    return pl.pallas_call(
        functools.partial(gather_up_kernel, group),
        grid_spec=pltpu.PrefetchScalarGridSpec(
            num_scalar_prefetch=2,
            grid=(n // group,),
            in_specs=[
                pl.BlockSpec((group, rows, lanes), lambda i, *_: (i, 0, 0)),
                pl.BlockSpec(theta2.shape, lambda i, *_: (0, 0)),
                pl.BlockSpec(phi.shape, lambda i, *_: (0, 0)),
                pl.BlockSpec(cs.shape, lambda i, *_: (0, 0, 0, 0, 0)),
            ],
            out_specs=[pl.BlockSpec(shape, lambda i, *_: (0, 0, 0, 0, 0))] * CHUNKS,
        ),
        out_shape=[jax.ShapeDtypeStruct(shape, F32)] * CHUNKS,
        compiler_params=pltpu.CompilerParams(vmem_limit_bytes=VMEM_BYTES),
    )(parent, octant, x, theta2, phi, cs)


def translate_kernel(chunk, far, kind, q_ref, trans_ref, upper_ref, *refs):
    rows_ref, plane_ref, buf, sem = refs[-4:]
    p = pl.program_id(0)
    count, many = pl.num_programs(0), far.shape[1]
    tl = q_ref.shape[2]
    part = pl.ds(chunk * buf.shape[2], buf.shape[2])

    def start(row, slot):
        for l in range(many):
            pltpu.make_async_copy(
                trans_ref.at[kind[row, l], part], buf.at[slot, l], sem.at[slot]
            ).start()

    @pl.when(p == 0)
    def _():
        start(0, 0)

    @pl.when(p + 1 < count)
    def _():
        start(p + 1, (p + 1) % 2)

    slot = p % 2
    pltpu.make_async_copy(trans_ref.at[pl.ds(0, many), part], buf.at[slot], sem.at[slot]).wait()
    for t in range(0, tl, 8):
        for h in range(2):
            re = im = None
            for l in range(many):
                f = far[p, l]
                q0 = q_ref[f, 0, t : t + 8, h * 128 : (h + 1) * 128]
                q1 = q_ref[f, 1, t : t + 8, h * 128 : (h + 1) * 128]
                a0 = buf[slot, l, pl.ds(t * 4 + h * 2, 8, stride=4), :]
                a1 = buf[slot, l, pl.ds(t * 4 + h * 2 + 1, 8, stride=4), :]
                r, i = a0 * q0 - a1 * q1, a0 * q1 + a1 * q0
                re = r if re is None else re + r
                im = i if im is None else im + i
            for c, total in ((0, re), (1, im)):
                where = pl.ds(t * 4 + h * 2 + c, 8, stride=4)
                total = total + upper_ref[0, where, :]
                rows_ref[0, where, :] = total
                plane_ref[0, c, t : t + 8, h * 128 : (h + 1) * 128] = total


def translate(chunk, q, trans, upper, far, kind, before):
    parents, all_rows, lanes = upper.shape
    rows = all_rows // CHUNKS
    _, _, tl, pc = q.shape
    many = far.shape[1]
    return pl.pallas_call(
        functools.partial(translate_kernel, chunk),
        grid_spec=pltpu.PrefetchScalarGridSpec(
            num_scalar_prefetch=2,
            grid=(parents,),
            in_specs=[
                pl.BlockSpec(q.shape, lambda i, *_: (0, 0, 0, 0)),
                pl.BlockSpec(memory_space=pl.ANY),
                pl.BlockSpec((1, rows, lanes), lambda i, *_: (i, chunk, 0)),
            ]
            + [pl.BlockSpec(memory_space=pl.ANY)] * len(before),
            out_specs=[
                pl.BlockSpec((1, rows, lanes), lambda i, *_: (i, chunk, 0)),
                pl.BlockSpec((1, 2, tl, pc), lambda i, *_: (i, 0, 0, 0)),
            ],
            scratch_shapes=[
                pltpu.VMEM((2, many, rows, lanes), F32),
                pltpu.SemaphoreType.DMA((2,)),
            ],
        ),
        out_shape=[
            jax.ShapeDtypeStruct((parents, all_rows, lanes), F32),
            jax.ShapeDtypeStruct((parents, 2, tl, pc), F32),
        ],
        compiler_params=pltpu.CompilerParams(vmem_limit_bytes=VMEM_BYTES),
        input_output_aliases={5: 0} if before else {},
    )(far, kind, q, trans, upper, *before)


def spread_down_kernel(group, parent, octant, *refs):
    in_refs, (theta_ref, phi_ref, cs_ref, out_ref, full) = refs[:-5], refs[-5:]
    step = pl.program_id(0)
    nd, tl = cs_ref.shape[0], cs_ref.shape[3]
    tlc = tl // len(in_refs)
    tc = nd * tl
    theta = split(theta_ref[...])
    phi = split(phi_ref[...])
    parts = []
    for g in range(group):
        p, o = parent[step * group + g], octant[step * group + g]
        for j in range(nd):
            for h, in_ref in enumerate(in_refs):
                first = j * tl + h * tlc
                re, im = in_ref[j, p, 0], in_ref[j, p, 1]
                c = cs_ref[j, 0, o, h * tlc : (h + 1) * tlc]
                s = cs_ref[j, 1, o, h * tlc : (h + 1) * tlc]
                full[g, first : first + tlc] = c * re + s * im
                full[g, tc + first : tc + first + tlc] = c * im - s * re
        parts.append(dot3(theta, split(full[g])))
    along = jnp.concatenate(parts, axis=0)
    out_ref[...] = dot3(split(along), phi).reshape(out_ref.shape)


def spread_down(incoming, theta2t, phit, cs, parent, octant):
    nd, _, _, tl, pc = cs.shape
    n = parent.shape[0]
    rows, lanes = theta2t.shape[0], phit.shape[1]
    group = 4
    return pl.pallas_call(
        functools.partial(spread_down_kernel, group),
        grid_spec=pltpu.PrefetchScalarGridSpec(
            num_scalar_prefetch=2,
            grid=(n // group,),
            in_specs=[
                *(pl.BlockSpec(x.shape, lambda i, *_: (0, 0, 0, 0, 0)) for x in incoming),
                pl.BlockSpec(theta2t.shape, lambda i, *_: (0, 0)),
                pl.BlockSpec(phit.shape, lambda i, *_: (0, 0)),
                pl.BlockSpec(cs.shape, lambda i, *_: (0, 0, 0, 0, 0)),
            ],
            out_specs=pl.BlockSpec((group, rows, lanes), lambda i, *_: (i, 0, 0)),
            scratch_shapes=[pltpu.VMEM((group, 2 * nd * tl, pc), F32)],
        ),
        out_shape=jax.ShapeDtypeStruct((n, rows, lanes), F32),
        compiler_params=pltpu.CompilerParams(vmem_limit_bytes=VMEM_BYTES),
    )(parent, octant, *incoming, theta2t, phit, cs)


def shards(
    fine_out,
    theta_interp,
    phi_interp,
    shift_phase,
    translation,
    upper_in,
    children,
    far_boxes,
    far_offsets,
):
    n = fine_out.shape[0]
    tc, tf = theta_interp.shape
    pc = phi_interp.shape[1]
    parents = children.shape[0]
    tl = shift_phase.shape[1] // pc
    nd = tc // tl
    flat = (children % (n * nd)).reshape(-1)
    own = lax.axis_index("dir") * n + jnp.arange(n, dtype=jnp.int32)
    slots = jnp.arange(flat.shape[0], dtype=jnp.int32)
    slot = jnp.sum(jnp.where(flat[None, :] == own[:, None], slots[None, :], 0), axis=1)
    parent, octant = slot // 8, slot % 8
    theta2 = (jnp.eye(2, dtype=F32)[:, None, None, :] * theta_interp[None, :, :, None]).reshape(
        2 * tc, 2 * tf
    )
    nb = lax.axis_size("box")
    phase = shift_phase.reshape(8 * tl, pc)
    share = 8 * tl // nb
    mine = lax.dynamic_slice_in_dim(phase, lax.axis_index("box") * share, share, axis=0)
    phases = lax.all_gather(mine, ("box", "dir"), axis=0, tiled=False)
    phases = phases.reshape(nb, nd, share, pc).transpose(1, 0, 2, 3).reshape(nd, 8, tl, pc)
    cs = jnp.stack([jnp.cos(phases), jnp.sin(phases)], axis=1)
    partials = gather_up(rows_view(fine_out), theta2, phi_interp, cs, parent, octant, parents)
    operators, upper = rows_view(translation), rows_view(upper_in)
    every_box = []
    for partial in partials:
        outgoing = lax.psum_scatter(
            partial.reshape((nd * parents * 2,) + partial.shape[3:]),
            "dir",
            scatter_dimension=0,
            tiled=True,
        ).reshape(partial.shape[1:])
        every_box.append(lax.all_gather(outgoing, "box", axis=0, tiled=True))
    before, incoming = (), []
    for chunk, sources in enumerate(every_box):
        rows, planes = translate(
            chunk, sources, operators, upper, far_boxes, far_offsets, before
        )
        before = (rows,)
        incoming.append(lax.all_gather(planes, "dir", axis=0))
    fine_in = spread_down(incoming, theta2.T, phi_interp.T, cs, parent, octant)
    return (rows_unview(rows), rows_unview(fine_in))


def solution(mesh):
    placed = (
        P(("box", "dir"), None, None),
        P(),
        P(),
        P(None, "dir"),
        P(None, None, "dir"),
        P("box", None, "dir"),
        P("box", None),
        P("box", None),
        P("box", None),
    )
    return jax.shard_map(
        shards,
        mesh=mesh,
        in_specs=placed,
        out_specs=(P("box", None, "dir"), P(("box", "dir"), None, None)),
        check_vma=False,
    )
```

```python
import functools

import jax
import jax.numpy as jnp
from jax import lax
from jax.experimental import pallas as pl
from jax.experimental.pallas import tpu as pltpu
from jax.sharding import PartitionSpec as P

F32, BF16 = jnp.float32, jnp.bfloat16
VMEM_BYTES = 52 * 1024 * 1024
CHUNKS = 2


def split(x):
    hi = x.astype(BF16)
    return hi, (x - hi.astype(F32)).astype(BF16)


def dot3(a, b):
    (ah, al), (bh, bl) = a, b
    d = functools.partial(jnp.dot, preferred_element_type=F32)
    return d(ah, bh) + (d(ah, bl) + d(al, bh))


def rows_view(x):
    n, _, k = x.shape
    return x.reshape(n, 2, k // 128, 128).transpose(0, 2, 1, 3).reshape(n, k // 64, 128)


def rows_unview(x):
    n, r, _ = x.shape
    return x.reshape(n, r // 2, 2, 128).transpose(0, 2, 1, 3).reshape(n, 2, r * 64)


def gather_up_kernel(group, parent, octant, x_ref, theta_ref, phi_ref, cs_ref, *out_refs):
    step = pl.program_id(0)
    nd, tl = cs_ref.shape[0], cs_ref.shape[3]
    tlc = tl // len(out_refs)
    tc = nd * tl

    @pl.when(step == 0)
    def _():
        for out_ref in out_refs:
            out_ref[...] = jnp.zeros_like(out_ref)

    theta = split(theta_ref[...])
    phi = split(phi_ref[...])
    rows = x_ref.shape[1]
    along = dot3(split(x_ref[...].reshape(group * rows, x_ref.shape[2])), phi)
    for g in range(group):
        p, o = parent[step * group + g], octant[step * group + g]
        full = dot3(theta, split(along[g * rows : (g + 1) * rows]))
        for j in range(nd):
            for h, out_ref in enumerate(out_refs):
                first = j * tl + h * tlc
                re = full[first : first + tlc]
                im = full[tc + first : tc + first + tlc]
                c = cs_ref[j, 0, o, h * tlc : (h + 1) * tlc]
                s = cs_ref[j, 1, o, h * tlc : (h + 1) * tlc]
                out_ref[j, p, 0] += c * re - s * im
                out_ref[j, p, 1] += s * re + c * im


def gather_up(x, theta2, phi, cs, parent, octant, parents):
    n, rows, lanes = x.shape
    nd, _, _, tl, pc = cs.shape
    shape = (nd, parents, 2, tl // CHUNKS, pc)
    group = 4
    return pl.pallas_call(
        functools.partial(gather_up_kernel, group),
        grid_spec=pltpu.PrefetchScalarGridSpec(
            num_scalar_prefetch=2,
            grid=(n // group,),
            in_specs=[
                pl.BlockSpec((group, rows, lanes), lambda i, *_: (i, 0, 0)),
                pl.BlockSpec(theta2.shape, lambda i, *_: (0, 0)),
                pl.BlockSpec(phi.shape, lambda i, *_: (0, 0)),
                pl.BlockSpec(cs.shape, lambda i, *_: (0, 0, 0, 0, 0)),
            ],
            out_specs=[pl.BlockSpec(shape, lambda i, *_: (0, 0, 0, 0, 0))] * CHUNKS,
        ),
        out_shape=[jax.ShapeDtypeStruct(shape, F32)] * CHUNKS,
        compiler_params=pltpu.CompilerParams(vmem_limit_bytes=VMEM_BYTES),
    )(parent, octant, x, theta2, phi, cs)


def translate_kernel(chunk, far, kind, q_ref, trans_ref, upper_ref, *refs):
    rows_ref, plane_ref, buf, sem = refs[-4:]
    p = pl.program_id(0)
    count, many = pl.num_programs(0), far.shape[1]
    tl = q_ref.shape[2]
    part = pl.ds(chunk * buf.shape[2], buf.shape[2])

    def start(row, slot):
        for l in range(many):
            pltpu.make_async_copy(
                trans_ref.at[kind[row, l], part], buf.at[slot, l], sem.at[slot]
            ).start()

    @pl.when(p == 0)
    def _():
        start(0, 0)

    @pl.when(p + 1 < count)
    def _():
        start(p + 1, (p + 1) % 2)

    slot = p % 2
    pltpu.make_async_copy(trans_ref.at[pl.ds(0, many), part], buf.at[slot], sem.at[slot]).wait()
    for t in range(0, tl, 8):
        for h in range(2):
            re = im = None
            for l in range(many):
                f = far[p, l]
                q0 = q_ref[f, 0, t : t + 8, h * 128 : (h + 1) * 128]
                q1 = q_ref[f, 1, t : t + 8, h * 128 : (h + 1) * 128]
                a0 = buf[slot, l, pl.ds(t * 4 + h * 2, 8, stride=4), :]
                a1 = buf[slot, l, pl.ds(t * 4 + h * 2 + 1, 8, stride=4), :]
                r, i = a0 * q0 - a1 * q1, a0 * q1 + a1 * q0
                re = r if re is None else re + r
                im = i if im is None else im + i
            for c, total in ((0, re), (1, im)):
                where = pl.ds(t * 4 + h * 2 + c, 8, stride=4)
                total = total + upper_ref[0, where, :]
                rows_ref[0, where, :] = total
                plane_ref[0, c, t : t + 8, h * 128 : (h + 1) * 128] = total


def translate(chunk, q, trans, upper, far, kind, before):
    parents, all_rows, lanes = upper.shape
    rows = all_rows // CHUNKS
    _, _, tl, pc = q.shape
    many = far.shape[1]
    return pl.pallas_call(
        functools.partial(translate_kernel, chunk),
        grid_spec=pltpu.PrefetchScalarGridSpec(
            num_scalar_prefetch=2,
            grid=(parents,),
            in_specs=[
                pl.BlockSpec(q.shape, lambda i, *_: (0, 0, 0, 0)),
                pl.BlockSpec(memory_space=pl.ANY),
                pl.BlockSpec((1, rows, lanes), lambda i, *_: (i, chunk, 0)),
            ]
            + [pl.BlockSpec(memory_space=pl.ANY)] * len(before),
            out_specs=[
                pl.BlockSpec((1, rows, lanes), lambda i, *_: (i, chunk, 0)),
                pl.BlockSpec((1, 2, tl, pc), lambda i, *_: (i, 0, 0, 0)),
            ],
            scratch_shapes=[
                pltpu.VMEM((2, many, rows, lanes), F32),
                pltpu.SemaphoreType.DMA((2,)),
            ],
        ),
        out_shape=[
            jax.ShapeDtypeStruct((parents, all_rows, lanes), F32),
            jax.ShapeDtypeStruct((parents, 2, tl, pc), F32),
        ],
        compiler_params=pltpu.CompilerParams(vmem_limit_bytes=VMEM_BYTES),
        input_output_aliases={5: 0} if before else {},
    )(far, kind, q, trans, upper, *before)


def spread_down_kernel(group, parent, octant, *refs):
    in_refs, (theta_ref, phi_ref, cs_ref, out_ref, full) = refs[:-5], refs[-5:]
    step = pl.program_id(0)
    nd, tl = cs_ref.shape[0], cs_ref.shape[3]
    tlc = tl // len(in_refs)
    tc = nd * tl
    theta = split(theta_ref[...])
    phi = split(phi_ref[...])
    parts = []
    for g in range(group):
        p, o = parent[step * group + g], octant[step * group + g]
        for j in range(nd):
            for h, in_ref in enumerate(in_refs):
                first = j * tl + h * tlc
                re, im = in_ref[j, p, 0], in_ref[j, p, 1]
                c = cs_ref[j, 0, o, h * tlc : (h + 1) * tlc]
                s = cs_ref[j, 1, o, h * tlc : (h + 1) * tlc]
                full[g, first : first + tlc] = c * re + s * im
                full[g, tc + first : tc + first + tlc] = c * im - s * re
        parts.append(dot3(theta, split(full[g])))
    along = jnp.concatenate(parts, axis=0)
    out_ref[...] = dot3(split(along), phi).reshape(out_ref.shape)


def spread_down(incoming, theta2t, phit, cs, parent, octant):
    nd, _, _, tl, pc = cs.shape
    n = parent.shape[0]
    rows, lanes = theta2t.shape[0], phit.shape[1]
    group = 4
    return pl.pallas_call(
        functools.partial(spread_down_kernel, group),
        grid_spec=pltpu.PrefetchScalarGridSpec(
            num_scalar_prefetch=2,
            grid=(n // group,),
            in_specs=[
                *(pl.BlockSpec(x.shape, lambda i, *_: (0, 0, 0, 0, 0)) for x in incoming),
                pl.BlockSpec(theta2t.shape, lambda i, *_: (0, 0)),
                pl.BlockSpec(phit.shape, lambda i, *_: (0, 0)),
                pl.BlockSpec(cs.shape, lambda i, *_: (0, 0, 0, 0, 0)),
            ],
            out_specs=pl.BlockSpec((group, rows, lanes), lambda i, *_: (i, 0, 0)),
            scratch_shapes=[pltpu.VMEM((group, 2 * nd * tl, pc), F32)],
        ),
        out_shape=jax.ShapeDtypeStruct((n, rows, lanes), F32),
        compiler_params=pltpu.CompilerParams(vmem_limit_bytes=VMEM_BYTES),
    )(parent, octant, *incoming, theta2t, phit, cs)


def box_bits():
    return range(lax.axis_size("box").bit_length() - 2, -1, -1)


def gather_box(x):
    nb = lax.axis_size("box")
    for bit in box_bits():
        other = lax.ppermute(x, "box", [(i, i ^ (1 << bit)) for i in range(nb)])
        x = jnp.concatenate([x, other], axis=0)
    return x


def box_place(box):
    apart = box ^ lax.axis_index("box")
    place = jnp.zeros_like(box)
    for stage, bit in enumerate(box_bits()):
        place = place + (((apart >> bit) & 1) << stage)
    return place


def shards(
    fine_out,
    theta_interp,
    phi_interp,
    shift_phase,
    translation,
    upper_in,
    children,
    far_boxes,
    far_offsets,
):
    n = fine_out.shape[0]
    tc, tf = theta_interp.shape
    pc = phi_interp.shape[1]
    parents = children.shape[0]
    tl = shift_phase.shape[1] // pc
    nd = tc // tl
    flat = (children % (n * nd)).reshape(-1)
    own = lax.axis_index("dir") * n + jnp.arange(n, dtype=jnp.int32)
    slots = jnp.arange(flat.shape[0], dtype=jnp.int32)
    slot = jnp.sum(jnp.where(flat[None, :] == own[:, None], slots[None, :], 0), axis=1)
    parent, octant = slot // 8, slot % 8
    theta2 = (jnp.eye(2, dtype=F32)[:, None, None, :] * theta_interp[None, :, :, None]).reshape(
        2 * tc, 2 * tf
    )
    phases = lax.all_gather(shift_phase.reshape(8, tl, pc), "dir", axis=0)
    cs = jnp.stack([jnp.cos(phases), jnp.sin(phases)], axis=1)
    partials = gather_up(rows_view(fine_out), theta2, phi_interp, cs, parent, octant, parents)
    operators, upper = rows_view(translation), rows_view(upper_in)
    every_box = []
    for partial in partials:
        outgoing = lax.psum_scatter(
            partial.reshape((nd * parents * 2,) + partial.shape[3:]),
            "dir",
            scatter_dimension=0,
            tiled=True,
        ).reshape(partial.shape[1:])
        if every_box:
            every_box[-1], outgoing = lax.optimization_barrier((every_box[-1], outgoing))
        every_box.append(gather_box(outgoing))
    sources_at = box_place(far_boxes // parents) * parents + far_boxes % parents
    before, incoming = (), []
    for chunk, sources in enumerate(every_box):
        rows, planes = translate(
            chunk, sources, operators, upper, sources_at, far_offsets, before
        )
        before = (rows,)
        incoming.append(lax.all_gather(planes, "dir", axis=0))
    fine_in = spread_down(incoming, theta2.T, phi_interp.T, cs, parent, octant)
    return (rows_unview(rows), rows_unview(fine_in))


def solution(mesh):
    placed = (
        P(("box", "dir"), None, None),
        P(),
        P(),
        P(None, "dir"),
        P(None, None, "dir"),
        P("box", None, "dir"),
        P("box", None),
        P("box", None),
        P("box", None),
    )
    return jax.shard_map(
        shards,
        mesh=mesh,
        in_specs=placed,
        out_specs=(P("box", None, "dir"), P(("box", "dir"), None, None)),
        check_vma=False,
    )
```
